32 devices in a mesh: sta: 8 (over z, x), slab: 4 (over y, core).
Axes of the slice: x: 2, y: 2, z: 4, core: 2. Of those that a mesh axis runs over, the one named last changes fastest.
Arguments:
- green_fields: bfloat16 [2, 16, 64, 4096], P(None, 'sta', 'slab'), may hold values from -6 to 6
- pair_list: int32 [64, 2], replicated, may hold values from 0 to 15
- pair_values: float32 [2, 64], replicated, may hold values from -6 to 6
- noise_map: float32 [64, 4096], P('slab'), may hold values from 0.1 to 1
- wave_square: float32 [64, 4096], P('slab'), may hold values from 0.1 to 1.5
- station_cell: int32 [16], P('sta'), may hold values from 0 to 262143
Outputs:
- adjoint_field: float32 [2, 16, 64, 4096], P(None, 'sta', 'slab')
The draws below stay inside these ranges and needn't reach their ends.
Inputs may be any that keep to these rules, and one draw needn't show every extreme that they name: `pair_list`: pairs may repeat and may name one station twice; repeated entries add up. `station_cell`: index = depth layer * 64 * 64 + lateral index; stations may share a cell.
All inputs are finite; a program needn't handle non-finite values.
Results may differ from the reference program's by a relative error of at most 0.004.
Values may be sent and summed in bfloat16 or wider, within the bound.
A program may use at most 64 MiB of HBM per device.

```python
import math
import jax
import jax.numpy as jnp
from jax import lax

GX = 64
GY = 64
SWEEPS = 6
STATIONS = 16
NZ = 64
PAIRS = 64


def with_ends(entries, stream_key, least, top_value):
    longest = entries.shape.index(max(entries.shape))
    spots = []
    for shift in (0, 1):
        where = [jax.random.randint(jax.random.fold_in(stream_key, axis), (), 0, length) for axis, length in enumerate(entries.shape)]
        where[longest] = (where[longest] + shift) % entries.shape[longest]
        spots.append(tuple(where))
    return entries.at[spots[0]].set(least).at[spots[1]].set(top_value)


def block_levels(key, shape, shards, least, largest):
    def one(dim, blocks):
        draws = jax.random.uniform(jax.random.fold_in(jax.random.fold_in(key, 6), dim), (blocks,), jnp.float32, least / len(shards), largest / len(shards))
        return jnp.repeat(jnp.exp(draws), shape[dim] // blocks).reshape((-1,) + (1,) * (len(shape) - dim - 1))

    factor_of = one(*shards[0])
    for cut in shards[1:]:
        factor_of = factor_of * one(*cut)
    return factor_of


def normal_values(stream_key, extent, deviation, most, pieces=(), kind=jnp.bfloat16):
    level = block_levels(stream_key, extent, pieces, -0.22, 0.18) if pieces else 1.0
    drawn = jax.random.normal(stream_key, extent, jnp.float32) * deviation * level
    return jnp.minimum(jnp.maximum(drawn, -most), most).astype(kind)


def setup_inputs(seed: int = 0) -> dict:
    key_of = jax.random.split(jax.random.key(seed), 7)
    return {
        "green_fields": normal_values(key_of[0], (2, STATIONS, NZ, GX * GY), 1.0, 6.0, ((1, 8), (2, 4))),
        "pair_list": with_ends(jax.random.randint(key_of[1], (PAIRS, 2), 0, STATIONS), jax.random.fold_in(key_of[1], 1), 0, STATIONS - 1).astype(jnp.int32),
        "pair_values": normal_values(key_of[2], (2, PAIRS), 1.0, 6.0, (), jnp.float32),
        "noise_map": jnp.clip(jnp.exp(math.log(1.0) - 2.3025851 * jax.random.uniform(key_of[3], (NZ, GX * GY), jnp.float32) ** block_levels(key_of[3], (NZ, GX * GY), ((0, 4),), -0.2, 0.2)), 0.1, 1.0),
        "wave_square": jnp.clip(jnp.exp(math.log(1.5) - 2.7080502 * jax.random.uniform(key_of[4], (NZ, GX * GY), jnp.float32) ** block_levels(key_of[4], (NZ, GX * GY), ((0, 4),), -0.2, 0.2)), 0.1, 1.5),
        "station_cell": with_ends(jax.random.randint(key_of[5], (STATIONS,), 0, NZ * GX * GY), jax.random.fold_in(key_of[5], 1), 0, (NZ * GX * GY) - 1).astype(jnp.int32),
    }


damping = 0.3
relaxation = 0.8
point_size = 2.0


def build_resid(pair_list, pair_values, count):
    labels = jnp.arange(count, dtype=jnp.int32)
    first = (pair_list[:, 0:1] == labels[None, :]).astype(jnp.float32)
    second = (pair_list[:, 1:2] == labels[None, :]).astype(jnp.float32)
    real_w = pair_values[0][:, None]
    imag_w = pair_values[1][:, None]
    highest = lax.Precision.HIGHEST
    resid_real = jnp.dot(first.T, real_w * second, precision=highest, preferred_element_type=jnp.float32) + jnp.dot(second.T, real_w * first, precision=highest, preferred_element_type=jnp.float32)
    resid_imag = jnp.dot(first.T, imag_w * second, precision=highest, preferred_element_type=jnp.float32) - jnp.dot(second.T, imag_w * first, precision=highest, preferred_element_type=jnp.float32)
    resid_real = resid_real.astype(jnp.bfloat16)
    resid_imag = resid_imag.astype(jnp.bfloat16)
    upper = jnp.concatenate([resid_real, -resid_imag], axis=1)
    lower = jnp.concatenate([resid_imag, resid_real], axis=1)
    return jnp.concatenate([upper, lower], axis=0)


def lateral(field, width_y):
    width = field.shape[-1]
    zeros_pad = [(0, 0)] * (field.ndim - 1)
    padded = jnp.pad(field, zeros_pad + [(width_y, width_y)])
    along_x = padded[..., :width] + padded[..., 2 * width_y:]
    column = jnp.arange(width, dtype=jnp.int32) % width_y
    stepped = jnp.pad(field, zeros_pad + [(1, 1)])
    left = stepped[..., :width] * (column != 0).astype(jnp.float32)
    right = stepped[..., 2:] * (column != width_y - 1).astype(jnp.float32)
    return along_x + left + right


def scales_from(wave):
    diag_real = 6.0 - wave
    denom = diag_real * diag_real + (damping * wave) * (damping * wave)
    return relaxation * diag_real / denom, relaxation * damping * wave / denom


def relax(padded, source, wave, scale_real, scale_imag, width_y):
    inner = padded[:, :, 1:-1]
    near = lateral(inner, width_y) + padded[:, :, :-2] + padded[:, :, 2:]
    real_in = inner[0]
    imag_in = inner[1]
    applied_real = 6.0 * real_in - near[0] - wave * (real_in - damping * imag_in)
    applied_imag = 6.0 * imag_in - near[1] - wave * (damping * real_in + imag_in)
    rest_real = source[0] - applied_real
    rest_imag = source[1] - applied_imag
    return jnp.stack([real_in + scale_real * rest_real - scale_imag * rest_imag, imag_in + scale_real * rest_imag + scale_imag * rest_real])


def reference(green_fields, pair_list, pair_values, noise_map, wave_square, station_cell):
    count = green_fields.shape[1]
    depth = green_fields.shape[2]
    cells = green_fields.shape[3]
    big = build_resid(pair_list, pair_values, count)
    flat = green_fields.reshape(2 * count, depth * cells)
    adjoint = jnp.dot(big, flat, preferred_element_type=jnp.float32).astype(jnp.bfloat16)
    adjoint = adjoint.reshape(2, count, depth, cells)
    scale_real, scale_imag = scales_from(wave_square)
    flat_cells = jnp.arange(depth * cells, dtype=jnp.int32)

    def one_station(index):
        part = lax.dynamic_index_in_dim(adjoint, index, 1, keepdims=True).astype(jnp.float32)
        spot = (flat_cells == station_cell[index]).astype(jnp.float32).reshape(1, depth, cells) * point_size
        source = noise_map[None, None] * part
        source = jnp.stack([source[0] + spot, source[1]])
        field = jnp.zeros((2, 1, depth, cells), jnp.float32)
        for repeat in range(SWEEPS):
            padded = jnp.pad(field, ((0, 0), (0, 0), (1, 1), (0, 0)))
            field = relax(padded, source, wave_square, scale_real, scale_imag, GY)
        return field[:, 0]

    result = lax.map(one_station, jnp.arange(count, dtype=jnp.int32))
    return jnp.transpose(result, (1, 0, 2, 3))
```

```python
import functools

import jax
import jax.numpy as jnp
from jax import lax
from jax.experimental import pallas as pl
from jax.experimental.pallas import tpu as pltpu
from jax.sharding import PartitionSpec as P

GY = 64
SWEEPS = 6
LANES = 128
HALO = 8
ROUNDS = 4

damping = 0.3
relaxation = 0.8
point_size = 2.0

MESH = pl.DeviceIdType.MESH
bf16 = jnp.bfloat16
f32 = jnp.float32


def partner(me, mask):
    other = me
    bit = 1
    while bit <= mask:
        if mask & bit:
            other = other + bit * (1 - 2 * ((me // bit) % 2))
        bit *= 2
    return other


def build_mixer(pairs_ref, values_ref, mixer, count, depth):
    number = pairs_ref.shape[0]
    eye = lax.broadcasted_iota(jnp.int32, (number, number), 0) == lax.broadcasted_iota(
        jnp.int32, (number, number), 1
    )
    pairs = pairs_ref[...]
    values = values_ref[...]
    columns = lax.broadcasted_iota(jnp.int32, (number, count), 1)
    rows = lax.broadcasted_iota(jnp.int32, (count, number), 0)

    def both(side):
        column = pairs[:, side : side + 1]
        row = jnp.sum(jnp.where(eye, column, 0), axis=0, keepdims=True)
        return (column == columns).astype(f32), (row == rows).astype(f32)

    first, first_t = both(0)
    second, second_t = both(1)
    parts = []
    for part, sign in ((0, 1.0), (1, -1.0)):
        weight = jnp.sum(jnp.where(eye, values[part : part + 1, :], 0.0), axis=1, keepdims=True)
        dot = functools.partial(
            jnp.dot, precision=lax.Precision.HIGHEST, preferred_element_type=f32
        )
        parts.append(
            (dot(first_t, weight * second) + sign * dot(second_t, weight * first)).astype(bf16)
        )
    size = count * depth
    block = min(size, 256)
    spread_t = (
        lax.broadcasted_iota(jnp.int32, (count, size), 1) // depth
        == lax.broadcasted_iota(jnp.int32, (count, size), 0)
    ).astype(bf16)
    for start in range(0, size, block):
        row_id = lax.broadcasted_iota(jnp.int32, (block, count), 0) + start
        spread = (row_id // depth == lax.broadcasted_iota(jnp.int32, (block, count), 1)).astype(
            bf16
        )
        same = (
            lax.broadcasted_iota(jnp.int32, (block, size), 0) % depth
            == lax.broadcasted_iota(jnp.int32, (block, size), 1) % depth
        )
        wide = []
        for part in parts:
            tall = jnp.dot(spread, part, preferred_element_type=f32).astype(bf16)
            full = jnp.dot(tall, spread_t, preferred_element_type=f32)
            wide.append(jnp.where(same, full, 0.0))
        here = slice(start, start + block)
        there = slice(size + start, size + start + block)
        mixer[here, :size] = wide[0].astype(bf16)
        mixer[here, size:] = (-wide[1]).astype(bf16)
        mixer[there, :size] = wide[1].astype(bf16)
        mixer[there, size:] = wide[0].astype(bf16)


def kernel(
    n,
    slabs,
    rounds,
    green,
    pairs_ref,
    values_ref,
    noise,
    wave,
    cell_ref,
    out,
    pieces,
    mixed,
    adjoint,
    mixer,
    edge_out,
    edge_in,
    map_in,
    source,
    scale_re,
    scale_im,
    field,
    send1,
    recv1,
    send2,
    recv2,
    send_edge,
    recv_edge,
    send_map,
    recv_map,
):
    me = lax.axis_index("sta")
    slab = lax.axis_index("slab")
    owned, depth, cells = green.shape[1], green.shape[2], green.shape[3]
    count = owned * n
    part = cells // rounds
    width = part // n
    tall = depth + 2 * HALO
    order = list(range(n - 1, 0, -1))
    above = slab + 1 < slabs
    below = slab > 0

    barrier = pltpu.get_barrier_semaphore()
    for mask in order:
        pl.semaphore_signal(
            barrier, inc=1, device_id={"sta": partner(me, mask)}, device_id_type=MESH
        )
    for step in (1, slabs - 1):
        pl.semaphore_signal(
            barrier, inc=1, device_id={"slab": lax.rem(slab + step, slabs)}, device_id_type=MESH
        )
    pl.semaphore_wait(barrier, n + 1)

    def lanes_of(turn, who):
        return pl.ds(pl.multiple_of(turn * part + who * width, width), width)

    def first_copy(turn, mask):
        other = partner(me, mask)
        return pltpu.make_async_remote_copy(
            src_ref=green.at[:, :, :, lanes_of(turn, other)],
            dst_ref=pieces.at[turn, :, pl.ds(me * owned, owned)],
            send_sem=send1.at[turn, mask],
            recv_sem=recv1.at[turn, mask],
            device_id={"sta": other},
            device_id_type=MESH,
        )

    def second_copy(turn, mask):
        other = partner(me, mask)
        return pltpu.make_async_remote_copy(
            src_ref=mixed.at[turn, :, pl.ds(other * owned, owned)],
            dst_ref=adjoint.at[:, :, :, lanes_of(turn, me)],
            send_sem=send2.at[turn, mask],
            recv_sem=recv2.at[turn, mask],
            device_id={"sta": other},
            device_id_type=MESH,
        )

    def map_copies(up):
        rows = slice(depth - HALO, depth) if up else slice(0, HALO)
        slot = 0 if up else 1
        target = slab + 1 if up else slab - 1
        return [
            pltpu.make_async_remote_copy(
                src_ref=ref.at[rows],
                dst_ref=map_in.at[slot, which],
                send_sem=send_map.at[slot, which],
                recv_sem=recv_map.at[slot, which],
                device_id={"slab": target},
                device_id_type=MESH,
            )
            for which, ref in enumerate((noise, wave))
        ]

    def edge_copy(up, turn):
        slot = 0 if up else 1
        target = slab + 1 if up else slab - 1
        here = slice(turn * part, (turn + 1) * part)
        return pltpu.make_async_remote_copy(
            src_ref=edge_out.at[slot, :, :, here],
            dst_ref=edge_in.at[slot, :, :, here],
            send_sem=send_edge.at[slot, turn],
            recv_sem=recv_edge.at[slot, turn],
            device_id={"slab": target},
            device_id_type=MESH,
        )

    def each(make, action):
        @pl.when(above)
        def _():
            action(make(True), make(False), True)

        @pl.when(below)
        def _():
            action(make(False), make(True), False)

    for turn in range(rounds):
        for mask in order:
            first_copy(turn, mask).start()

    def start_maps(mine, theirs, up):
        for copy in mine:
            copy.start()

    each(map_copies, start_maps)

    for turn in range(rounds):
        pieces[turn, :, pl.ds(me * owned, owned)] = green[:, :, :, lanes_of(turn, me)]
    build_mixer(pairs_ref, values_ref, mixer, count, depth)

    def wait_maps(mine, theirs, up):
        for copy in mine:
            copy.wait_send()
        for copy in theirs:
            copy.wait_recv()

    each(map_copies, wait_maps)

    def tile_of(t):
        return pl.ds(pl.multiple_of(t * LANES, LANES), LANES)

    def extend(low, middle, high):
        return jnp.concatenate([jnp.where(below, low, 0.0), middle, jnp.where(above, high, 0.0)], 0)

    def scales(t, carry):
        tile = tile_of(t)
        inside = extend(
            jnp.ones((HALO, LANES), f32), jnp.ones((depth, LANES), f32), jnp.ones((HALO, LANES), f32)
        )
        square = extend(map_in[0, 1, :, tile], wave[:, tile], map_in[1, 1, :, tile])
        diag = 6.0 - square
        lossy = damping * square
        factor = inside * relaxation / (diag * diag + lossy * lossy)
        scale_re[:, tile] = diag * factor
        scale_im[:, tile] = lossy * factor
        return carry

    lax.fori_loop(0, cells // LANES, scales, 0)
    for buffer in range(2):
        for k in range(2 * owned):
            field[buffer, k, :, :LANES] = jnp.zeros((tall, LANES), f32)
            field[buffer, k, :, LANES + cells :] = jnp.zeros((tall, LANES), f32)

    size = 2 * count * depth
    block = min(size, 256)
    for turn in range(rounds):
        for mask in order:
            first_copy(turn, mask).wait_recv()
        stacked = pieces[turn].reshape(size, width)
        for start in range(0, size, block):
            product = jnp.dot(
                mixer[start : start + block, :], stacked, preferred_element_type=f32
            ).astype(bf16)
            side = start // (count * depth)
            station = (start % (count * depth)) // depth
            mixed[turn, side, station : station + block // depth] = product.reshape(
                block // depth, depth, width
            )
        for mask in order:
            second_copy(turn, mask).start()
        adjoint[:, :, :, lanes_of(turn, me)] = mixed[turn, :, pl.ds(me * owned, owned)]

    columns = lax.broadcasted_iota(jnp.int32, (1, LANES), 1)
    not_first = (columns % GY) != 0
    not_last = (columns % GY) != GY - 1
    upper_half = columns >= GY
    per_part = part // LANES

    def pack(t, carry):
        tile = tile_of(t)
        for k in range(owned):
            re = adjoint[0, k, :, tile].astype(f32)
            im = adjoint[1, k, :, tile].astype(f32)
            edge_out[0, k, :, tile] = jnp.concatenate(
                [re[depth - HALO :], im[depth - HALO :]], 0
            ).astype(bf16)
            edge_out[1, k, :, tile] = jnp.concatenate([re[:HALO], im[:HALO]], 0).astype(bf16)
        return carry

    spot_rows = (
        (slab * depth - HALO + lax.broadcasted_iota(jnp.int32, (tall, LANES), 0)) * cells
        + lax.broadcasted_iota(jnp.int32, (tall, LANES), 1)
    )

    def begin(t, carry):
        tile = tile_of(t)
        shifted = tile_of(t + 1)
        power = extend(map_in[0, 0, :, tile], noise[:, tile], map_in[1, 0, :, tile])
        s_re = scale_re[:, tile]
        s_im = scale_im[:, tile]
        ids = spot_rows + t * LANES
        for k in range(owned):
            low = edge_in[0, k, :, tile].astype(f32)
            high = edge_in[1, k, :, tile].astype(f32)
            re = extend(low[:HALO], adjoint[0, k, :, tile].astype(f32), high[:HALO])
            im = extend(low[HALO:], adjoint[1, k, :, tile].astype(f32), high[HALO:])
            re = power * re + jnp.where(ids == cell_ref[k], point_size, 0.0)
            im = power * im
            source[2 * k, :, tile] = re
            source[2 * k + 1, :, tile] = im
            field[0, 2 * k, :, shifted] = s_re * re - s_im * im
            field[0, 2 * k + 1, :, shifted] = s_re * im + s_im * re
        return carry

    def near(old, k, t):
        v = field[old, k, :, tile_of(t + 1)]
        before = field[old, k, :, tile_of(t)]
        after = field[old, k, :, tile_of(t + 2)]
        along_x = pltpu.roll(v + jnp.where(upper_half, before, after), GY, 1)
        left = jnp.where(not_first, pltpu.roll(v, 1, 1), 0.0)
        right = jnp.where(not_last, pltpu.roll(v, LANES - 1, 1), 0.0)
        along_z = pltpu.roll(v, 1, 0) + pltpu.roll(v, tall - 1, 0)
        return v, along_x + left + right + along_z

    kept = 1.0 - relaxation

    def sweep(old, final, t, carry):
        tile = tile_of(t)
        s_re = scale_re[:, tile]
        s_im = scale_im[:, tile]
        for k in range(owned):
            v_re, n_re = near(old, 2 * k, t)
            v_im, n_im = near(old, 2 * k + 1, t)
            n_re = n_re + source[2 * k, :, tile]
            n_im = n_im + source[2 * k + 1, :, tile]
            re = kept * v_re + (s_re * n_re - s_im * n_im)
            im = kept * v_im + (s_re * n_im + s_im * n_re)
            if final:
                out[0, k, :, tile] = re[HALO : HALO + depth]
                out[1, k, :, tile] = im[HALO : HALO + depth]
            else:
                field[1 - old, 2 * k, :, tile_of(t + 1)] = re
                field[1 - old, 2 * k + 1, :, tile_of(t + 1)] = im
        return carry

    def compute(turn):
        def wait_edge(mine, theirs, up):
            theirs.wait_recv()

        each(lambda up: edge_copy(up, turn), wait_edge)
        lax.fori_loop(turn * per_part, (turn + 1) * per_part, begin, 0)
        for number in range(1, SWEEPS):
            low = 0 if turn == 0 else max(turn * per_part - number, 0)
            high = cells // LANES if turn == rounds - 1 else max((turn + 1) * per_part - number, 0)
            if high > low:
                old = (number - 1) % 2
                lax.fori_loop(
                    low, high, functools.partial(sweep, old, number == SWEEPS - 1), 0
                )

    for turn in range(rounds):
        for mask in order:
            second_copy(turn, mask).wait_recv()
        lax.fori_loop(turn * per_part, (turn + 1) * per_part, pack, 0)

        def start_edge(mine, theirs, up):
            mine.start()

        each(lambda up: edge_copy(up, turn), start_edge)
        if turn > 0:
            compute(turn - 1)
    compute(rounds - 1)

    for turn in range(rounds):
        for mask in order:
            first_copy(turn, mask).wait_send()
            second_copy(turn, mask).wait_send()

        def end_edge(mine, theirs, up):
            mine.wait_send()

        each(lambda up: edge_copy(up, turn), end_edge)


def local(n, slabs, green_fields, pair_list, pair_values, noise_map, wave_square, station_cell):
    _, owned, depth, cells = green_fields.shape
    count = owned * n
    rounds = min(ROUNDS, cells // (n * LANES))
    width = cells // (n * rounds)
    tall = depth + 2 * HALO
    size = 2 * count * depth
    vmem = pl.BlockSpec(memory_space=pltpu.VMEM)
    dma = pltpu.SemaphoreType.DMA
    return pl.pallas_call(
        functools.partial(kernel, n, slabs, rounds),
        out_shape=jax.ShapeDtypeStruct((2, owned, depth, cells), f32),
        in_specs=[vmem] * 5 + [pl.BlockSpec(memory_space=pltpu.SMEM)],
        out_specs=vmem,
        scratch_shapes=[
            pltpu.VMEM((rounds, 2, count, depth, width), bf16),
            pltpu.VMEM((rounds, 2, count, depth, width), bf16),
            pltpu.VMEM((2, owned, depth, cells), bf16),
            pltpu.VMEM((size, size), bf16),
            pltpu.VMEM((2, owned, 2 * HALO, cells), bf16),
            pltpu.VMEM((2, owned, 2 * HALO, cells), bf16),
            pltpu.VMEM((2, 2, HALO, cells), f32),
            pltpu.VMEM((2 * owned, tall, cells), f32),
            pltpu.VMEM((tall, cells), f32),
            pltpu.VMEM((tall, cells), f32),
            pltpu.VMEM((2, 2 * owned, tall, cells + 2 * LANES), f32),
            dma((rounds, n)),
            dma((rounds, n)),
            dma((rounds, n)),
            dma((rounds, n)),
            dma((2, rounds)),
            dma((2, rounds)),
            dma((2, 2)),
            dma((2, 2)),
        ],
        compiler_params=pltpu.CompilerParams(
            collective_id=0, has_side_effects=True, vmem_limit_bytes=48 * 1024 * 1024
        ),
    )(green_fields, pair_list, pair_values, noise_map, wave_square, station_cell)


def solution(mesh):
    placed = (P(None, "sta", "slab", None), P(), P(), P("slab", None), P("slab", None), P("sta"))
    return jax.shard_map(
        functools.partial(local, mesh.shape["sta"], mesh.shape["slab"]),
        mesh=mesh,
        in_specs=placed,
        out_specs=P(None, "sta", "slab", None),
        check_vma=False,
    )
```

```python
import functools

import jax
import jax.numpy as jnp
from jax import lax
from jax.experimental import pallas as pl
from jax.experimental.pallas import tpu as pltpu
from jax.sharding import PartitionSpec as P

GY = 64
SWEEPS = 6
LANES = 128
HALO = 8
ROUNDS = 4
GROUP = 2

damping = 0.3
relaxation = 0.8
point_size = 2.0

MESH = pl.DeviceIdType.MESH
bf16 = jnp.bfloat16
f32 = jnp.float32


def partner(me, mask):
    other = me
    bit = 1
    while bit <= mask:
        if mask & bit:
            other = other + bit * (1 - 2 * ((me // bit) % 2))
        bit *= 2
    return other


def build_mixer(pairs_ref, values_ref, mixer, count, depth):
    number = pairs_ref.shape[1]
    eye = lax.broadcasted_iota(jnp.int32, (number, number), 0) == lax.broadcasted_iota(
        jnp.int32, (number, number), 1
    )
    pairs = pairs_ref[...]
    values = values_ref[...]
    columns = lax.broadcasted_iota(jnp.int32, (number, count), 1)
    rows = lax.broadcasted_iota(jnp.int32, (count, number), 0)

    def both(side):
        row = pairs[side : side + 1, :]
        column = jnp.sum(jnp.where(eye, row, 0), axis=1, keepdims=True)
        return (column == columns).astype(f32), (row == rows).astype(f32)

    first, first_t = both(0)
    second, second_t = both(1)
    parts = []
    for part, sign in ((0, 1.0), (1, -1.0)):
        weight = jnp.sum(jnp.where(eye, values[part : part + 1, :], 0.0), axis=1, keepdims=True)
        dot = functools.partial(
            jnp.dot, precision=lax.Precision.HIGHEST, preferred_element_type=f32
        )
        parts.append(
            (dot(first_t, weight * second) + sign * dot(second_t, weight * first)).astype(bf16)
        )
    size = count * depth
    block = min(size, 256)
    spread_t = (
        lax.broadcasted_iota(jnp.int32, (count, size), 1) // depth
        == lax.broadcasted_iota(jnp.int32, (count, size), 0)
    ).astype(bf16)
    for start in range(0, size, block):
        row_id = lax.broadcasted_iota(jnp.int32, (block, count), 0) + start
        spread = (row_id // depth == lax.broadcasted_iota(jnp.int32, (block, count), 1)).astype(
            bf16
        )
        same = (
            lax.broadcasted_iota(jnp.int32, (block, size), 0) % depth
            == lax.broadcasted_iota(jnp.int32, (block, size), 1) % depth
        )
        wide = []
        for part in parts:
            tall = jnp.dot(spread, part, preferred_element_type=f32).astype(bf16)
            full = jnp.dot(tall, spread_t, preferred_element_type=f32)
            wide.append(jnp.where(same, full, 0.0))
        here = slice(start, start + block)
        there = slice(size + start, size + start + block)
        mixer[here, :size] = wide[0].astype(bf16)
        mixer[here, size:] = (-wide[1]).astype(bf16)
        mixer[there, :size] = wide[1].astype(bf16)
        mixer[there, size:] = wide[0].astype(bf16)


def kernel(
    n,
    slabs,
    rounds,
    green,
    pairs_ref,
    values_ref,
    noise_hbm,
    wave_hbm,
    cell_ref,
    out,
    noise,
    wave,
    pieces,
    mixed,
    adjoint,
    mixer,
    edge_out,
    edge_in,
    map_in,
    source,
    source_edge,
    scale_re,
    scale_im,
    map_scale,
    field_a,
    field_b,
    send1,
    recv1,
    send2,
    recv2,
    send_edge,
    recv_edge,
    send_map,
    recv_map,
    own_sem,
    local_sem,
):
    me = lax.axis_index("sta")
    slab = lax.axis_index("slab")
    owned, depth, cells = green.shape[1], green.shape[2], green.shape[3]
    count = owned * n
    part = cells // rounds
    width = part // n
    tall = depth + HALO
    half = HALO // 2
    fields = (field_a, field_b)
    order = list(range(n - 1, 0, -1))
    above = slab + 1 < slabs
    below = slab > 0

    local_maps = [
        pltpu.make_async_copy(noise_hbm, noise, local_sem.at[0]),
        pltpu.make_async_copy(wave_hbm, wave, local_sem.at[1]),
    ]
    barrier = pltpu.get_barrier_semaphore()
    for mask in order:
        pl.semaphore_signal(
            barrier, inc=1, device_id={"sta": partner(me, mask)}, device_id_type=MESH
        )
    for step in (1, slabs - 1):
        pl.semaphore_signal(
            barrier, inc=1, device_id={"slab": lax.rem(slab + step, slabs)}, device_id_type=MESH
        )
    pl.semaphore_wait(barrier, n + 1)

    def lanes_of(turn, who):
        return pl.ds(pl.multiple_of(turn * part + who * width, width), width)

    def first_copy(turn, mask):
        other = partner(me, mask)
        return pltpu.make_async_remote_copy(
            src_ref=green.at[:, :, :, lanes_of(turn, other)],
            dst_ref=pieces.at[turn, :, pl.ds(me * owned, owned)],
            send_sem=send1.at[turn, mask],
            recv_sem=recv1.at[turn, mask],
            device_id={"sta": other},
            device_id_type=MESH,
        )

    def second_copy(turn, mask):
        other = partner(me, mask)
        return pltpu.make_async_remote_copy(
            src_ref=mixed.at[turn, :, pl.ds(other * owned, owned)],
            dst_ref=adjoint.at[:, :, :, lanes_of(turn, me)],
            send_sem=send2.at[turn, mask],
            recv_sem=recv2.at[turn, mask],
            device_id={"sta": other},
            device_id_type=MESH,
        )

    def map_copies(up):
        rows = slice(depth - HALO, depth) if up else slice(0, HALO)
        slot = 0 if up else 1
        target = slab + 1 if up else slab - 1
        return [
            pltpu.make_async_remote_copy(
                src_ref=ref.at[rows],
                dst_ref=map_in.at[slot, which],
                send_sem=send_map.at[slot, which],
                recv_sem=recv_map.at[slot, which],
                device_id={"slab": target},
                device_id_type=MESH,
            )
            for which, ref in enumerate((noise_hbm, wave_hbm))
        ]

    def edge_copy(up, turn):
        slot = 0 if up else 1
        target = slab + 1 if up else slab - 1
        here = slice(turn * part, (turn + 1) * part)
        return pltpu.make_async_remote_copy(
            src_ref=edge_out.at[slot, :, :, here],
            dst_ref=edge_in.at[slot, :, :, here],
            send_sem=send_edge.at[slot, turn],
            recv_sem=recv_edge.at[slot, turn],
            device_id={"slab": target},
            device_id_type=MESH,
        )

    def each(make, action):
        @pl.when(above)
        def _():
            action(make(True), make(False), True)

        @pl.when(below)
        def _():
            action(make(False), make(True), False)

    for turn in range(rounds):
        for mask in order:
            first_copy(turn, mask).start()

    def start_maps(mine, theirs, up):
        for copy in mine:
            copy.start()

    each(map_copies, start_maps)

    own = [
        pltpu.make_async_copy(
            green.at[:, :, :, lanes_of(turn, me)],
            pieces.at[turn, :, pl.ds(me * owned, owned)],
            own_sem.at[turn],
        )
        for turn in range(rounds)
    ]
    for copy in own + local_maps:
        copy.start()
    build_mixer(pairs_ref, values_ref, mixer, count, depth)

    def wait_maps(mine, theirs, up):
        for copy in mine:
            copy.wait_send()
        for copy in theirs:
            copy.wait_recv()

    each(map_copies, wait_maps)
    for copy in local_maps:
        copy.wait()

    def tile_of(t):
        return pl.ds(pl.multiple_of(t * LANES, LANES), LANES)

    def scale_of(square):
        diag = 6.0 - square
        lossy = damping * square
        factor = relaxation / (diag * diag + lossy * lossy)
        return diag * factor, lossy * factor

    edge_rows = lax.broadcasted_iota(jnp.int32, (HALO, LANES), 0)
    is_high = edge_rows < half

    def scales(t, carry):
        tile = tile_of(t)
        s_re, s_im = scale_of(wave[:, tile])
        scale_re[:depth, tile] = s_re
        scale_im[:depth, tile] = s_im
        for slot, there in ((0, below), (1, above)):
            l_re, l_im = scale_of(jnp.where(there, map_in[slot, 1, :, tile], 0.0))
            map_scale[slot, 0, :, tile] = jnp.where(there, l_re, 0.0)
            map_scale[slot, 1, :, tile] = jnp.where(there, l_im, 0.0)
        scale_re[depth:, tile] = jnp.where(
            is_high, map_scale[1, 0, :, tile], map_scale[0, 0, :, tile]
        )
        scale_im[depth:, tile] = jnp.where(
            is_high, map_scale[1, 1, :, tile], map_scale[0, 1, :, tile]
        )
        return carry

    lax.fori_loop(0, cells // LANES, scales, 0)
    for ref in fields:
        for k in range(2 * owned):
            ref[k, :, :LANES] = jnp.zeros((tall, LANES), f32)
            ref[k, :, LANES + cells :] = jnp.zeros((tall, LANES), f32)

    size = 2 * count * depth
    block = min(size, 256)
    for turn in range(rounds):
        own[turn].wait()
        for mask in order:
            first_copy(turn, mask).wait_recv()
        stacked = pieces[turn].reshape(size, width)
        for start in range(0, size, block):
            product = jnp.dot(
                mixer[start : start + block, :], stacked, preferred_element_type=f32
            ).astype(bf16)
            side = start // (count * depth)
            station = (start % (count * depth)) // depth
            mixed[turn, side, station : station + block // depth] = product.reshape(
                block // depth, depth, width
            )
        for mask in order:
            second_copy(turn, mask).start()
        adjoint[:, :, :, lanes_of(turn, me)] = mixed[turn, :, pl.ds(me * owned, owned)]

    columns = lax.broadcasted_iota(jnp.int32, (1, LANES), 1)
    not_first = (columns % GY) != 0
    not_last = (columns % GY) != GY - 1
    upper_half = columns >= GY
    per_part = part // LANES

    def pack(t):
        tile = tile_of(t)
        for k in range(owned):
            re = adjoint[0, k, :, tile].astype(f32)
            im = adjoint[1, k, :, tile].astype(f32)
            edge_out[0, k, :, tile] = jnp.concatenate(
                [re[depth - HALO :], im[depth - HALO :]], 0
            ).astype(bf16)
            edge_out[1, k, :, tile] = jnp.concatenate([re[:HALO], im[:HALO]], 0).astype(bf16)

    def ids_from(row, rows):
        return (slab * depth + row + lax.broadcasted_iota(jnp.int32, (rows, LANES), 0)) * cells + (
            lax.broadcasted_iota(jnp.int32, (rows, LANES), 1)
        )

    ids_main = ids_from(0, depth)
    ids_low = ids_from(-HALO, HALO)
    ids_high = ids_from(depth, HALO)

    def begin(t):
        tile = tile_of(t)
        shifted = tile_of(t + 1)
        step = t * LANES
        for k in range(owned):
            low = edge_in[0, k, :, tile].astype(f32)
            high = edge_in[1, k, :, tile].astype(f32)

            def start(power, re, im, ids, s_re, s_im):
                re = power * re + jnp.where(ids + step == cell_ref[k], point_size, 0.0)
                im = power * im
                return re, im, s_re * re - s_im * im, s_re * im + s_im * re

            def outer(slot, there, values, ids):
                return start(
                    jnp.where(there, map_in[slot, 0, :, tile], 0.0),
                    jnp.where(there, values[:HALO], 0.0),
                    jnp.where(there, values[HALO:], 0.0),
                    ids,
                    map_scale[slot, 0, :, tile],
                    map_scale[slot, 1, :, tile],
                )

            main = start(
                noise[:, tile],
                adjoint[0, k, :, tile].astype(f32),
                adjoint[1, k, :, tile].astype(f32),
                ids_main,
                scale_re[:depth, tile],
                scale_im[:depth, tile],
            )
            under = outer(0, below, low, ids_low)
            over = outer(1, above, high, ids_high)
            for c in range(2):
                kc = 2 * k + c
                source[kc, :depth, tile] = main[c]
                edge = jnp.where(is_high, over[c], under[c])
                source[kc, depth:, tile] = edge
                fields[0][kc, :depth, shifted] = main[2 + c]
                f_over, f_under = over[2 + c], under[2 + c]
                fields[0][kc, depth:, shifted] = jnp.where(is_high, f_over, f_under)
                fifth_over = pltpu.roll(f_over, HALO - 1, 0) - pltpu.roll(f_under, HALO - 1, 0)
                fifth_under = pltpu.roll(f_under, 1, 0) - pltpu.roll(f_over, 1, 0)
                fix = jnp.where(edge_rows == half - 1, fifth_over, 0.0) + jnp.where(
                    edge_rows == half, fifth_under, 0.0
                )
                source_edge[kc, :, tile] = edge + fix

    def near(old, k, t):
        v = fields[old][k, :, tile_of(t + 1)]
        before = fields[old][k, :, tile_of(t)]
        after = fields[old][k, :, tile_of(t + 2)]
        along_x = pltpu.roll(v + jnp.where(upper_half, before, after), GY, 1)
        left = jnp.where(not_first, pltpu.roll(v, 1, 1), 0.0)
        right = jnp.where(not_last, pltpu.roll(v, LANES - 1, 1), 0.0)
        along_z = pltpu.roll(v, 1, 0) + pltpu.roll(v, tall - 1, 0)
        return v, along_x + left + right + along_z

    kept = 1.0 - relaxation

    def sweep(number, t):
        old = (number - 1) % 2
        final = number == SWEEPS - 1
        rows = depth if final else tall
        tile = tile_of(t)
        s_re = scale_re[:rows, tile]
        s_im = scale_im[:rows, tile]

        def pulled(kc):
            v, n = near(old, kc, t)
            if number == 1:
                added = jnp.concatenate([source[kc, :depth, tile], source_edge[kc, :, tile]], 0)
            else:
                added = source[kc, :rows, tile]
            return v[:rows], n[:rows] + added

        for k in range(owned):
            v_re, n_re = pulled(2 * k)
            v_im, n_im = pulled(2 * k + 1)
            re = kept * v_re + (s_re * n_re - s_im * n_im)
            im = kept * v_im + (s_re * n_im + s_im * n_re)
            if final:
                out[0, k, :, tile] = re
                out[1, k, :, tile] = im
            else:
                fields[1 - old][2 * k, :, tile_of(t + 1)] = re
                fields[1 - old][2 * k + 1, :, tile_of(t + 1)] = im

    def run(low, high, work):
        groups = (high - low) // GROUP

        def many(g, carry):
            for j in range(GROUP):
                work(low + g * GROUP + j)
            return carry

        if groups:
            lax.fori_loop(0, groups, many, 0)
        for t in range(low + groups * GROUP, high):
            work(t)

    def compute(turn):
        def wait_edge(mine, theirs, up):
            theirs.wait_recv()

        each(lambda up: edge_copy(up, turn), wait_edge)
        run(turn * per_part, (turn + 1) * per_part, begin)
        for number in range(1, SWEEPS):
            low = 0 if turn == 0 else max(turn * per_part - number, 0)
            high = cells // LANES if turn == rounds - 1 else max((turn + 1) * per_part - number, 0)
            if high > low:
                run(low, high, functools.partial(sweep, number))

    for turn in range(rounds):
        for mask in order:
            second_copy(turn, mask).wait_recv()
        run(turn * per_part, (turn + 1) * per_part, pack)

        def start_edge(mine, theirs, up):
            mine.start()

        each(lambda up: edge_copy(up, turn), start_edge)
        if turn > 0:
            compute(turn - 1)
    compute(rounds - 1)

    for turn in range(rounds):
        for mask in order:
            first_copy(turn, mask).wait_send()
            second_copy(turn, mask).wait_send()

        def end_edge(mine, theirs, up):
            mine.wait_send()

        each(lambda up: edge_copy(up, turn), end_edge)


def local(n, slabs, green_fields, pair_list, pair_values, noise_map, wave_square, station_cell):
    _, owned, depth, cells = green_fields.shape
    count = owned * n
    rounds = min(ROUNDS, cells // (n * LANES))
    width = cells // (n * rounds)
    tall = depth + HALO
    size = 2 * count * depth
    vmem = pl.BlockSpec(memory_space=pltpu.VMEM)
    hbm = pl.BlockSpec(memory_space=pl.ANY)
    dma = pltpu.SemaphoreType.DMA
    return pl.pallas_call(
        functools.partial(kernel, n, slabs, rounds),
        out_shape=jax.ShapeDtypeStruct((2, owned, depth, cells), f32),
        in_specs=[hbm, vmem, vmem, hbm, hbm, pl.BlockSpec(memory_space=pltpu.SMEM)],
        out_specs=vmem,
        scratch_shapes=[
            pltpu.VMEM((depth, cells), f32),
            pltpu.VMEM((depth, cells), f32),
            pltpu.VMEM((rounds, 2, count, depth, width), bf16),
            pltpu.VMEM((rounds, 2, count, depth, width), bf16),
            pltpu.VMEM((2, owned, depth, cells), bf16),
            pltpu.VMEM((size, size), bf16),
            pltpu.VMEM((2, owned, 2 * HALO, cells), bf16),
            pltpu.VMEM((2, owned, 2 * HALO, cells), bf16),
            pltpu.VMEM((2, 2, HALO, cells), f32),
            pltpu.VMEM((2 * owned, tall, cells), f32),
            pltpu.VMEM((2 * owned, HALO, cells), f32),
            pltpu.VMEM((tall, cells), f32),
            pltpu.VMEM((tall, cells), f32),
            pltpu.VMEM((2, 2, HALO, cells), f32),
            pltpu.VMEM((2 * owned, tall, cells + 2 * LANES), f32),
            pltpu.VMEM((2 * owned, tall, cells + 2 * LANES), f32),
            dma((rounds, n)),
            dma((rounds, n)),
            dma((rounds, n)),
            dma((rounds, n)),
            dma((2, rounds)),
            dma((2, rounds)),
            dma((2, 2)),
            dma((2, 2)),
            dma((rounds,)),
            dma((2,)),
        ],
        compiler_params=pltpu.CompilerParams(
            collective_id=0, has_side_effects=True, vmem_limit_bytes=48 * 1024 * 1024
        ),
    )(green_fields, pair_list.T, pair_values, noise_map, wave_square, station_cell)


def solution(mesh):
    placed = (P(None, "sta", "slab", None), P(), P(), P("slab", None), P("slab", None), P("sta"))
    return jax.shard_map(
        functools.partial(local, mesh.shape["sta"], mesh.shape["slab"]),
        mesh=mesh,
        in_specs=placed,
        out_specs=P(None, "sta", "slab", None),
        check_vma=False,
    )
```

```python
import functools

import jax
import jax.numpy as jnp
from jax import lax
from jax.experimental import pallas as pl
from jax.experimental.pallas import tpu as pltpu
from jax.sharding import PartitionSpec as P

GY = 64
SWEEPS = 6
LANES = 128
HALO = 8
ROUNDS = 4
GROUP = 4

damping = 0.3
relaxation = 0.8
point_size = 2.0

MESH = pl.DeviceIdType.MESH
bf16 = jnp.bfloat16
f32 = jnp.float32


def partner(me, mask):
    other = me
    bit = 1
    while bit <= mask:
        if mask & bit:
            other = other + bit * (1 - 2 * ((me // bit) % 2))
        bit *= 2
    return other


def build_mixer(pairs_ref, values_ref, mixer, count, depth):
    number = pairs_ref.shape[1]
    eye = lax.broadcasted_iota(jnp.int32, (number, number), 0) == lax.broadcasted_iota(
        jnp.int32, (number, number), 1
    )
    pairs = pairs_ref[...]
    values = values_ref[...]
    columns = lax.broadcasted_iota(jnp.int32, (number, count), 1)
    rows = lax.broadcasted_iota(jnp.int32, (count, number), 0)

    def both(side):
        row = pairs[side : side + 1, :]
        column = jnp.sum(jnp.where(eye, row, 0), axis=1, keepdims=True)
        return (column == columns).astype(f32), (row == rows).astype(f32)

    first, first_t = both(0)
    second, second_t = both(1)
    parts = []
    for part, sign in ((0, 1.0), (1, -1.0)):
        weight = jnp.sum(jnp.where(eye, values[part : part + 1, :], 0.0), axis=1, keepdims=True)
        dot = functools.partial(
            jnp.dot, precision=lax.Precision.HIGHEST, preferred_element_type=f32
        )
        parts.append(
            (dot(first_t, weight * second) + sign * dot(second_t, weight * first)).astype(bf16)
        )
    size = count * depth
    block = min(size, 256)
    spread_t = (
        lax.broadcasted_iota(jnp.int32, (count, size), 1) // depth
        == lax.broadcasted_iota(jnp.int32, (count, size), 0)
    ).astype(bf16)
    for start in range(0, size, block):
        row_id = lax.broadcasted_iota(jnp.int32, (block, count), 0) + start
        spread = (row_id // depth == lax.broadcasted_iota(jnp.int32, (block, count), 1)).astype(
            bf16
        )
        same = (
            lax.broadcasted_iota(jnp.int32, (block, size), 0) % depth
            == lax.broadcasted_iota(jnp.int32, (block, size), 1) % depth
        )
        wide = []
        for part in parts:
            tall = jnp.dot(spread, part, preferred_element_type=f32).astype(bf16)
            full = jnp.dot(tall, spread_t, preferred_element_type=f32)
            wide.append(jnp.where(same, full, 0.0))
        here = slice(start, start + block)
        there = slice(size + start, size + start + block)
        mixer[here, :size] = wide[0].astype(bf16)
        mixer[here, size:] = (-wide[1]).astype(bf16)
        mixer[there, :size] = wide[1].astype(bf16)
        mixer[there, size:] = wide[0].astype(bf16)


def kernel(
    n,
    slabs,
    rounds,
    green,
    pairs_hbm,
    values_hbm,
    noise_hbm,
    wave_hbm,
    cell_hbm,
    out,
    pairs_ref,
    values_ref,
    cell_ref,
    noise,
    wave,
    pieces,
    mixed,
    adjoint,
    mixer,
    edge_out,
    edge_in,
    map_in,
    source,
    source_edge,
    scale_re,
    scale_im,
    map_scale,
    field_a,
    field_b,
    send1,
    recv1,
    send2,
    recv2,
    send_edge,
    recv_edge,
    send_map,
    recv_map,
    own_sem,
    local_sem,
):
    me = lax.axis_index("sta")
    slab = lax.axis_index("slab")
    owned, depth, cells = green.shape[1], green.shape[2], green.shape[3]
    count = owned * n
    part = cells // rounds
    width = part // n
    tall = depth + HALO
    half = HALO // 2
    fields = (field_a, field_b)
    order = list(range(n - 1, 0, -1))
    above = slab + 1 < slabs
    below = slab > 0

    local_maps = [
        pltpu.make_async_copy(noise_hbm, noise, local_sem.at[0]),
        pltpu.make_async_copy(wave_hbm, wave, local_sem.at[1]),
    ]
    small = [
        pltpu.make_async_copy(pairs_hbm, pairs_ref, local_sem.at[2]),
        pltpu.make_async_copy(values_hbm, values_ref, local_sem.at[3]),
        pltpu.make_async_copy(cell_hbm, cell_ref, local_sem.at[4]),
    ]
    for copy in small:
        copy.start()
    barrier = pltpu.get_barrier_semaphore()
    for mask in order:
        pl.semaphore_signal(
            barrier, inc=1, device_id={"sta": partner(me, mask)}, device_id_type=MESH
        )
    for step in (1, slabs - 1):
        pl.semaphore_signal(
            barrier, inc=1, device_id={"slab": lax.rem(slab + step, slabs)}, device_id_type=MESH
        )
    pl.semaphore_wait(barrier, n + 1)

    def lanes_of(turn, who):
        return pl.ds(pl.multiple_of(turn * part + who * width, width), width)

    def first_copy(turn, mask):
        other = partner(me, mask)
        return pltpu.make_async_remote_copy(
            src_ref=green.at[:, :, :, lanes_of(turn, other)],
            dst_ref=pieces.at[turn, :, pl.ds(me * owned, owned)],
            send_sem=send1.at[turn, mask],
            recv_sem=recv1.at[turn, mask],
            device_id={"sta": other},
            device_id_type=MESH,
        )

    def second_copy(turn, mask):
        other = partner(me, mask)
        return pltpu.make_async_remote_copy(
            src_ref=mixed.at[turn, :, pl.ds(other * owned, owned)],
            dst_ref=adjoint.at[turn, me],
            send_sem=send2.at[turn, mask],
            recv_sem=recv2.at[turn, mask],
            device_id={"sta": other},
            device_id_type=MESH,
        )

    def map_copies(up):
        rows = slice(depth - HALO, depth) if up else slice(0, HALO)
        slot = 0 if up else 1
        target = slab + 1 if up else slab - 1
        return [
            pltpu.make_async_remote_copy(
                src_ref=ref.at[rows],
                dst_ref=map_in.at[slot, which],
                send_sem=send_map.at[slot, which],
                recv_sem=recv_map.at[slot, which],
                device_id={"slab": target},
                device_id_type=MESH,
            )
            for which, ref in enumerate((noise_hbm, wave_hbm))
        ]

    def edge_copy(up, turn):
        slot = 0 if up else 1
        target = slab + 1 if up else slab - 1
        here = slice(turn * part, (turn + 1) * part)
        return pltpu.make_async_remote_copy(
            src_ref=edge_out.at[slot, :, :, here],
            dst_ref=edge_in.at[slot, :, :, here],
            send_sem=send_edge.at[slot, turn],
            recv_sem=recv_edge.at[slot, turn],
            device_id={"slab": target},
            device_id_type=MESH,
        )

    def each(make, action):
        @pl.when(above)
        def _():
            action(make(True), make(False), True)

        @pl.when(below)
        def _():
            action(make(False), make(True), False)

    for turn in range(rounds):
        for mask in order:
            first_copy(turn, mask).start()

    def start_maps(mine, theirs, up):
        for copy in mine:
            copy.start()

    each(map_copies, start_maps)

    own = [
        pltpu.make_async_copy(
            green.at[:, :, :, lanes_of(turn, me)],
            pieces.at[turn, :, pl.ds(me * owned, owned)],
            own_sem.at[turn],
        )
        for turn in range(rounds)
    ]
    for copy in own + local_maps:
        copy.start()
    for copy in small:
        copy.wait()
    build_mixer(pairs_ref, values_ref, mixer, count, depth)

    def wait_maps(mine, theirs, up):
        for copy in mine:
            copy.wait_send()
        for copy in theirs:
            copy.wait_recv()

    each(map_copies, wait_maps)
    for copy in local_maps:
        copy.wait()

    def tile_of(t):
        return pl.ds(pl.multiple_of(t * LANES, LANES), LANES)

    def scale_of(square):
        diag = 6.0 - square
        lossy = damping * square
        factor = relaxation / (diag * diag + lossy * lossy)
        return diag * factor, lossy * factor

    edge_rows = lax.broadcasted_iota(jnp.int32, (HALO, LANES), 0)
    is_high = edge_rows < half

    def scales(t, carry):
        tile = tile_of(t)
        s_re, s_im = scale_of(wave[:, tile])
        scale_re[:depth, tile] = s_re
        scale_im[:depth, tile] = s_im
        for slot, there in ((0, below), (1, above)):
            l_re, l_im = scale_of(jnp.where(there, map_in[slot, 1, :, tile], 0.0))
            map_scale[slot, 0, :, tile] = jnp.where(there, l_re, 0.0)
            map_scale[slot, 1, :, tile] = jnp.where(there, l_im, 0.0)
        scale_re[depth:, tile] = jnp.where(
            is_high, map_scale[1, 0, :, tile], map_scale[0, 0, :, tile]
        )
        scale_im[depth:, tile] = jnp.where(
            is_high, map_scale[1, 1, :, tile], map_scale[0, 1, :, tile]
        )
        return carry

    lax.fori_loop(0, cells // LANES, scales, 0)
    for ref in fields:
        for k in range(2 * owned):
            ref[k, :, :LANES] = jnp.zeros((tall, LANES), f32)
            ref[k, :, LANES + cells :] = jnp.zeros((tall, LANES), f32)

    size = 2 * count * depth
    block = min(size, 256)
    for turn in range(rounds):
        own[turn].wait()
        for mask in order:
            first_copy(turn, mask).wait_recv()
        stacked = pieces[turn].reshape(size, width)
        for start in range(0, size, block):
            product = jnp.dot(
                mixer[start : start + block, :], stacked, preferred_element_type=f32
            ).astype(bf16)
            side = start // (count * depth)
            station = (start % (count * depth)) // depth
            mixed[turn, side, station : station + block // depth] = product.reshape(
                block // depth, depth, width
            )
        for mask in order:
            second_copy(turn, mask).start()
        adjoint[turn, me] = mixed[turn, :, pl.ds(me * owned, owned)]

    columns = lax.broadcasted_iota(jnp.int32, (1, LANES), 1)
    not_first = (columns % GY) != 0
    not_last = (columns % GY) != GY - 1
    upper_half = columns >= GY
    per_part = part // LANES

    def adjoint_at(turn, t, c, k):
        who = (t - turn * per_part) // (width // LANES)
        return adjoint[turn, who, c, k, :, tile_of(t % (width // LANES))].astype(f32)

    def pack(turn, t):
        tile = tile_of(t)
        for k in range(owned):
            re = adjoint_at(turn, t, 0, k)
            im = adjoint_at(turn, t, 1, k)
            edge_out[0, k, :, tile] = jnp.concatenate(
                [re[depth - HALO :], im[depth - HALO :]], 0
            ).astype(bf16)
            edge_out[1, k, :, tile] = jnp.concatenate([re[:HALO], im[:HALO]], 0).astype(bf16)

    def ids_from(row, rows):
        return (slab * depth + row + lax.broadcasted_iota(jnp.int32, (rows, LANES), 0)) * cells + (
            lax.broadcasted_iota(jnp.int32, (rows, LANES), 1)
        )

    ids_main = ids_from(0, depth)
    ids_low = ids_from(-HALO, HALO)
    ids_high = ids_from(depth, HALO)

    def begin(turn, t):
        tile = tile_of(t)
        shifted = tile_of(t + 1)
        step = t * LANES
        for k in range(owned):
            low = edge_in[0, k, :, tile].astype(f32)
            high = edge_in[1, k, :, tile].astype(f32)

            def start(power, re, im, ids, s_re, s_im):
                re = power * re + jnp.where(ids + step == cell_ref[:, k : k + 1], point_size, 0.0)
                im = power * im
                return re, im, s_re * re - s_im * im, s_re * im + s_im * re

            def outer(slot, there, values, ids):
                return start(
                    jnp.where(there, map_in[slot, 0, :, tile], 0.0),
                    jnp.where(there, values[:HALO], 0.0),
                    jnp.where(there, values[HALO:], 0.0),
                    ids,
                    map_scale[slot, 0, :, tile],
                    map_scale[slot, 1, :, tile],
                )

            main = start(
                noise[:, tile],
                adjoint_at(turn, t, 0, k),
                adjoint_at(turn, t, 1, k),
                ids_main,
                scale_re[:depth, tile],
                scale_im[:depth, tile],
            )
            under = outer(0, below, low, ids_low)
            over = outer(1, above, high, ids_high)
            for c in range(2):
                kc = 2 * k + c
                source[kc, :depth, tile] = main[c]
                edge = jnp.where(is_high, over[c], under[c])
                source[kc, depth:, tile] = edge
                fields[0][kc, :depth, shifted] = main[2 + c]
                f_over, f_under = over[2 + c], under[2 + c]
                fields[0][kc, depth:, shifted] = jnp.where(is_high, f_over, f_under)
                fifth_over = pltpu.roll(f_over, HALO - 1, 0) - pltpu.roll(f_under, HALO - 1, 0)
                fifth_under = pltpu.roll(f_under, 1, 0) - pltpu.roll(f_over, 1, 0)
                fix = jnp.where(edge_rows == half - 1, fifth_over, 0.0) + jnp.where(
                    edge_rows == half, fifth_under, 0.0
                )
                source_edge[kc, :, tile] = edge + fix

    def near(before, v, after):
        along_x = pltpu.roll(v + jnp.where(upper_half, before, after), GY, 1)
        left = jnp.where(not_first, pltpu.roll(v, 1, 1), 0.0)
        right = jnp.where(not_last, pltpu.roll(v, LANES - 1, 1), 0.0)
        along_z = pltpu.roll(v, 1, 0) + pltpu.roll(v, tall - 1, 0)
        return along_x + left + right + along_z

    kept = 1.0 - relaxation

    def sweep(number, start, tiles):
        old = (number - 1) % 2
        final = number == SWEEPS - 1
        rows = depth if final else tall
        s_re = [scale_re[:rows, tile_of(start + j)] for j in range(tiles)]
        s_im = [scale_im[:rows, tile_of(start + j)] for j in range(tiles)]

        def pulled(kc):
            v = [fields[old][kc, :, tile_of(start + j)] for j in range(tiles + 2)]
            gives = []
            for j in range(tiles):
                tile = tile_of(start + j)
                if number == 1:
                    added = jnp.concatenate([source[kc, :depth, tile], source_edge[kc, :, tile]], 0)
                else:
                    added = source[kc, :rows, tile]
                n = near(v[j], v[j + 1], v[j + 2])
                gives.append((kept * v[j + 1][:rows], n[:rows] + added))
            return gives

        for k in range(owned):
            real = pulled(2 * k)
            imag = pulled(2 * k + 1)
            new = []
            for j in range(tiles):
                (v_re, n_re), (v_im, n_im) = real[j], imag[j]
                new.append(
                    (
                        v_re + (s_re[j] * n_re - s_im[j] * n_im),
                        v_im + (s_re[j] * n_im + s_im[j] * n_re),
                    )
                )
            for j in range(tiles):
                for c in range(2):
                    if final:
                        out[c, k, :, tile_of(start + j)] = new[j][c]
                    else:
                        fields[1 - old][2 * k + c, :, tile_of(start + j + 1)] = new[j][c]

    def run_sweep(low, high, number):
        groups = (high - low) // GROUP

        def many(g, carry):
            sweep(number, low + g * GROUP, GROUP)
            return carry

        if groups:
            lax.fori_loop(0, groups, many, 0)
        rest = (high - low) % GROUP
        if rest:
            sweep(number, high - rest, rest)

    def run(low, high, work, size):
        def many(g, carry):
            for j in range(size):
                work(low + g * size + j)
            return carry

        lax.fori_loop(0, (high - low) // size, many, 0)

    def compute(turn):
        def wait_edge(mine, theirs, up):
            theirs.wait_recv()

        each(lambda up: edge_copy(up, turn), wait_edge)
        run(turn * per_part, (turn + 1) * per_part, functools.partial(begin, turn), 2)
        for number in range(1, SWEEPS):
            low = 0 if turn == 0 else max(turn * per_part - number, 0)
            high = cells // LANES if turn == rounds - 1 else max((turn + 1) * per_part - number, 0)
            if high > low:
                run_sweep(low, high, number)

    for turn in range(rounds):
        for mask in order:
            second_copy(turn, mask).wait_recv()
        run(turn * per_part, (turn + 1) * per_part, functools.partial(pack, turn), 4)

        def start_edge(mine, theirs, up):
            mine.start()

        each(lambda up: edge_copy(up, turn), start_edge)
        if turn > 0:
            compute(turn - 1)
    compute(rounds - 1)

    for turn in range(rounds):
        for mask in order:
            first_copy(turn, mask).wait_send()
            second_copy(turn, mask).wait_send()

        def end_edge(mine, theirs, up):
            mine.wait_send()

        each(lambda up: edge_copy(up, turn), end_edge)


def local(n, slabs, green_fields, pair_list, pair_values, noise_map, wave_square, station_cell):
    _, owned, depth, cells = green_fields.shape
    count = owned * n
    rounds = min(ROUNDS, cells // (n * LANES))
    width = cells // (n * rounds)
    tall = depth + HALO
    size = 2 * count * depth
    vmem = pl.BlockSpec(memory_space=pltpu.VMEM)
    hbm = pl.BlockSpec(memory_space=pltpu.HBM)
    dma = pltpu.SemaphoreType.DMA
    return pl.pallas_call(
        functools.partial(kernel, n, slabs, rounds),
        out_shape=jax.ShapeDtypeStruct((2, owned, depth, cells), f32),
        in_specs=[hbm] * 6,
        out_specs=vmem,
        scratch_shapes=[
            pltpu.VMEM(pair_list.shape[::-1], jnp.int32),
            pltpu.VMEM(pair_values.shape, f32),
            pltpu.VMEM((1, owned), jnp.int32),
            pltpu.VMEM((depth, cells), f32),
            pltpu.VMEM((depth, cells), f32),
            pltpu.VMEM((rounds, 2, count, depth, width), bf16),
            pltpu.VMEM((rounds, 2, count, depth, width), bf16),
            pltpu.VMEM((rounds, n, 2, owned, depth, width), bf16),
            pltpu.VMEM((size, size), bf16),
            pltpu.VMEM((2, owned, 2 * HALO, cells), bf16),
            pltpu.VMEM((2, owned, 2 * HALO, cells), bf16),
            pltpu.VMEM((2, 2, HALO, cells), f32),
            pltpu.VMEM((2 * owned, tall, cells), f32),
            pltpu.VMEM((2 * owned, HALO, cells), f32),
            pltpu.VMEM((tall, cells), f32),
            pltpu.VMEM((tall, cells), f32),
            pltpu.VMEM((2, 2, HALO, cells), f32),
            pltpu.VMEM((2 * owned, tall, cells + 2 * LANES), f32),
            pltpu.VMEM((2 * owned, tall, cells + 2 * LANES), f32),
            dma((rounds, n)),
            dma((rounds, n)),
            dma((rounds, n)),
            dma((rounds, n)),
            dma((2, rounds)),
            dma((2, rounds)),
            dma((2, 2)),
            dma((2, 2)),
            dma((rounds,)),
            dma((5,)),
        ],
        compiler_params=pltpu.CompilerParams(
            collective_id=0, has_side_effects=True, vmem_limit_bytes=62 * 1024 * 1024
        ),
    )(green_fields, pair_list.T, pair_values, noise_map, wave_square, station_cell[None, :])


def solution(mesh):
    placed = (P(None, "sta", "slab", None), P(), P(), P("slab", None), P("slab", None), P("sta"))
    return jax.shard_map(
        functools.partial(local, mesh.shape["sta"], mesh.shape["slab"]),
        mesh=mesh,
        in_specs=placed,
        out_specs=P(None, "sta", "slab", None),
        check_vma=False,
    )
```

```python
import functools

import jax
import jax.numpy as jnp
from jax import lax
from jax.experimental import pallas as pl
from jax.experimental.pallas import tpu as pltpu
from jax.sharding import PartitionSpec as P

GY = 64
SWEEPS = 6
LANES = 128
HALO = 8
ROUNDS = 2
GROUP = 4

damping = 0.3
relaxation = 0.8
point_size = 2.0

MESH = pl.DeviceIdType.MESH
bf16 = jnp.bfloat16
f32 = jnp.float32


def partner(me, mask):
    other = me
    bit = 1
    while bit <= mask:
        if mask & bit:
            other = other + bit * (1 - 2 * ((me // bit) % 2))
        bit *= 2
    return other


def build_mixer(pairs_ref, values_ref, mixer, count, depth):
    number = pairs_ref.shape[1]
    eye = lax.broadcasted_iota(jnp.int32, (number, number), 0) == lax.broadcasted_iota(
        jnp.int32, (number, number), 1
    )
    pairs = pairs_ref[...]
    values = values_ref[...]
    columns = lax.broadcasted_iota(jnp.int32, (number, count), 1)
    rows = lax.broadcasted_iota(jnp.int32, (count, number), 0)

    def both(side):
        row = pairs[side : side + 1, :]
        column = jnp.sum(jnp.where(eye, row, 0), axis=1, keepdims=True)
        return (column == columns).astype(f32), (row == rows).astype(f32)

    first, first_t = both(0)
    second, second_t = both(1)
    parts = []
    for part, sign in ((0, 1.0), (1, -1.0)):
        weight = jnp.sum(jnp.where(eye, values[part : part + 1, :], 0.0), axis=1, keepdims=True)
        dot = functools.partial(
            jnp.dot, precision=lax.Precision.HIGHEST, preferred_element_type=f32
        )
        parts.append(
            (dot(first_t, weight * second) + sign * dot(second_t, weight * first)).astype(bf16)
        )
    size = count * depth
    block = min(size, 256)
    spread_t = (
        lax.broadcasted_iota(jnp.int32, (count, size), 1) // depth
        == lax.broadcasted_iota(jnp.int32, (count, size), 0)
    ).astype(bf16)
    for start in range(0, size, block):
        row_id = lax.broadcasted_iota(jnp.int32, (block, count), 0) + start
        spread = (row_id // depth == lax.broadcasted_iota(jnp.int32, (block, count), 1)).astype(
            bf16
        )
        same = (
            lax.broadcasted_iota(jnp.int32, (block, size), 0) % depth
            == lax.broadcasted_iota(jnp.int32, (block, size), 1) % depth
        )
        wide = []
        for part in parts:
            tall = jnp.dot(spread, part, preferred_element_type=f32).astype(bf16)
            full = jnp.dot(tall, spread_t, preferred_element_type=f32)
            wide.append(jnp.where(same, full, 0.0))
        here = slice(start, start + block)
        there = slice(size + start, size + start + block)
        mixer[here, :size] = wide[0].astype(bf16)
        mixer[here, size:] = (-wide[1]).astype(bf16)
        mixer[there, :size] = wide[1].astype(bf16)
        mixer[there, size:] = wide[0].astype(bf16)


def kernel(
    n,
    slabs,
    rounds,
    green,
    pairs_hbm,
    values_hbm,
    noise_hbm,
    wave_hbm,
    cell_hbm,
    out,
    pairs_ref,
    values_ref,
    cell_ref,
    noise,
    wave,
    pieces,
    mixed,
    adjoint,
    mixer,
    edge_out,
    edge_in,
    map_in,
    source,
    source_edge,
    scale_re,
    scale_im,
    map_scale,
    field_a,
    field_b,
    send1,
    recv1,
    send2,
    recv2,
    send_edge,
    recv_edge,
    send_map,
    recv_map,
    own_sem,
    local_sem,
):
    me = lax.axis_index("sta")
    slab = lax.axis_index("slab")
    owned, depth, cells = green.shape[1], green.shape[2], green.shape[3]
    count = owned * n
    part = cells // rounds
    width = part // n
    tall = depth + HALO
    half = HALO // 2
    fields = (field_a, field_b)
    order = list(range(n - 1, 0, -1))
    above = slab + 1 < slabs
    below = slab > 0

    local_maps = [
        pltpu.make_async_copy(noise_hbm, noise, local_sem.at[0]),
        pltpu.make_async_copy(wave_hbm, wave, local_sem.at[1]),
    ]
    small = [
        pltpu.make_async_copy(pairs_hbm, pairs_ref, local_sem.at[2]),
        pltpu.make_async_copy(values_hbm, values_ref, local_sem.at[3]),
        pltpu.make_async_copy(cell_hbm, cell_ref, local_sem.at[4]),
    ]
    for copy in small:
        copy.start()
    barrier = pltpu.get_barrier_semaphore()
    for mask in order:
        pl.semaphore_signal(
            barrier, inc=1, device_id={"sta": partner(me, mask)}, device_id_type=MESH
        )
    for step in (1, slabs - 1):
        pl.semaphore_signal(
            barrier, inc=1, device_id={"slab": lax.rem(slab + step, slabs)}, device_id_type=MESH
        )
    pl.semaphore_wait(barrier, n + 1)

    def lanes_of(turn, who):
        return pl.ds(pl.multiple_of(turn * part + who * width, width), width)

    def first_copy(turn, mask):
        other = partner(me, mask)
        return pltpu.make_async_remote_copy(
            src_ref=green.at[:, :, :, lanes_of(turn, other)],
            dst_ref=pieces.at[turn, :, pl.ds(me * owned, owned)],
            send_sem=send1.at[turn, mask],
            recv_sem=recv1.at[turn, mask],
            device_id={"sta": other},
            device_id_type=MESH,
        )

    def second_copy(turn, mask):
        other = partner(me, mask)
        return pltpu.make_async_remote_copy(
            src_ref=mixed.at[turn, :, pl.ds(other * owned, owned)],
            dst_ref=adjoint.at[turn, me],
            send_sem=send2.at[turn, mask],
            recv_sem=recv2.at[turn, mask],
            device_id={"sta": other},
            device_id_type=MESH,
        )

    def map_copies(up):
        rows = slice(depth - HALO, depth) if up else slice(0, HALO)
        slot = 0 if up else 1
        target = slab + 1 if up else slab - 1
        return [
            pltpu.make_async_remote_copy(
                src_ref=ref.at[rows],
                dst_ref=map_in.at[slot, which],
                send_sem=send_map.at[slot, which],
                recv_sem=recv_map.at[slot, which],
                device_id={"slab": target},
                device_id_type=MESH,
            )
            for which, ref in enumerate((noise_hbm, wave_hbm))
        ]

    def edge_copy(up, turn):
        slot = 0 if up else 1
        target = slab + 1 if up else slab - 1
        here = slice(turn * part, (turn + 1) * part)
        return pltpu.make_async_remote_copy(
            src_ref=edge_out.at[slot, :, :, here],
            dst_ref=edge_in.at[slot, :, :, here],
            send_sem=send_edge.at[slot, turn],
            recv_sem=recv_edge.at[slot, turn],
            device_id={"slab": target},
            device_id_type=MESH,
        )

    def each(make, action):
        @pl.when(above)
        def _():
            action(make(True), make(False), True)

        @pl.when(below)
        def _():
            action(make(False), make(True), False)

    for turn in range(rounds):
        for mask in order:
            first_copy(turn, mask).start()

    def start_maps(mine, theirs, up):
        for copy in mine:
            copy.start()

    each(map_copies, start_maps)

    own = [
        pltpu.make_async_copy(
            green.at[:, :, :, lanes_of(turn, me)],
            pieces.at[turn, :, pl.ds(me * owned, owned)],
            own_sem.at[turn],
        )
        for turn in range(rounds)
    ]
    for copy in own + local_maps:
        copy.start()
    for copy in small:
        copy.wait()
    build_mixer(pairs_ref, values_ref, mixer, count, depth)

    def wait_maps(mine, theirs, up):
        for copy in mine:
            copy.wait_send()
        for copy in theirs:
            copy.wait_recv()

    each(map_copies, wait_maps)
    for copy in local_maps:
        copy.wait()

    def tile_of(t):
        return pl.ds(pl.multiple_of(t * LANES, LANES), LANES)

    def scale_of(square):
        diag = 6.0 - square
        lossy = damping * square
        factor = relaxation / (diag * diag + lossy * lossy)
        return diag * factor, lossy * factor

    edge_rows = lax.broadcasted_iota(jnp.int32, (HALO, LANES), 0)
    is_high = edge_rows < half

    def scales(t, carry):
        tile = tile_of(t)
        s_re, s_im = scale_of(wave[:, tile])
        scale_re[:depth, tile] = s_re
        scale_im[:depth, tile] = s_im
        for slot, there in ((0, below), (1, above)):
            l_re, l_im = scale_of(jnp.where(there, map_in[slot, 1, :, tile], 0.0))
            map_scale[slot, 0, :, tile] = jnp.where(there, l_re, 0.0)
            map_scale[slot, 1, :, tile] = jnp.where(there, l_im, 0.0)
        scale_re[depth:, tile] = jnp.where(
            is_high, map_scale[1, 0, :, tile], map_scale[0, 0, :, tile]
        )
        scale_im[depth:, tile] = jnp.where(
            is_high, map_scale[1, 1, :, tile], map_scale[0, 1, :, tile]
        )
        return carry

    lax.fori_loop(0, cells // LANES, scales, 0)
    for ref in fields:
        for k in range(2 * owned):
            ref[k, :, :LANES] = jnp.zeros((tall, LANES), f32)
            ref[k, :, LANES + cells :] = jnp.zeros((tall, LANES), f32)

    size = 2 * count * depth
    block = min(size, 256)
    for turn in range(rounds):
        own[turn].wait()
        for mask in order:
            first_copy(turn, mask).wait_recv()
        stacked = pieces[turn].reshape(size, width)
        for start in range(0, size, block):
            product = jnp.dot(
                mixer[start : start + block, :], stacked, preferred_element_type=f32
            ).astype(bf16)
            side = start // (count * depth)
            station = (start % (count * depth)) // depth
            mixed[turn, side, station : station + block // depth] = product.reshape(
                block // depth, depth, width
            )
        for mask in order:
            second_copy(turn, mask).start()
        adjoint[turn, me] = mixed[turn, :, pl.ds(me * owned, owned)]

    columns = lax.broadcasted_iota(jnp.int32, (1, LANES), 1)
    not_first = (columns % GY) != 0
    not_last = (columns % GY) != GY - 1
    upper_half = columns >= GY
    per_part = part // LANES

    def adjoint_at(turn, t, c, k):
        who = (t - turn * per_part) // (width // LANES)
        return adjoint[turn, who, c, k, :, tile_of(t % (width // LANES))].astype(f32)

    def pack(turn, t):
        tile = tile_of(t)
        for k in range(owned):
            re = adjoint_at(turn, t, 0, k)
            im = adjoint_at(turn, t, 1, k)
            edge_out[0, k, :, tile] = jnp.concatenate(
                [re[depth - HALO :], im[depth - HALO :]], 0
            ).astype(bf16)
            edge_out[1, k, :, tile] = jnp.concatenate([re[:HALO], im[:HALO]], 0).astype(bf16)

    def ids_from(row, rows):
        return (slab * depth + row + lax.broadcasted_iota(jnp.int32, (rows, LANES), 0)) * cells + (
            lax.broadcasted_iota(jnp.int32, (rows, LANES), 1)
        )

    ids_main = ids_from(0, depth)
    ids_low = ids_from(-HALO, HALO)
    ids_high = ids_from(depth, HALO)

    def begin(turn, t):
        tile = tile_of(t)
        shifted = tile_of(t + 1)
        step = t * LANES
        for k in range(owned):
            low = edge_in[0, k, :, tile].astype(f32)
            high = edge_in[1, k, :, tile].astype(f32)

            def start(power, re, im, ids, s_re, s_im):
                re = power * re + jnp.where(ids + step == cell_ref[:, k : k + 1], point_size, 0.0)
                im = power * im
                return re, im, s_re * re - s_im * im, s_re * im + s_im * re

            def outer(slot, there, values, ids):
                return start(
                    jnp.where(there, map_in[slot, 0, :, tile], 0.0),
                    jnp.where(there, values[:HALO], 0.0),
                    jnp.where(there, values[HALO:], 0.0),
                    ids,
                    map_scale[slot, 0, :, tile],
                    map_scale[slot, 1, :, tile],
                )

            main = start(
                noise[:, tile],
                adjoint_at(turn, t, 0, k),
                adjoint_at(turn, t, 1, k),
                ids_main,
                scale_re[:depth, tile],
                scale_im[:depth, tile],
            )
            under = outer(0, below, low, ids_low)
            over = outer(1, above, high, ids_high)
            for c in range(2):
                kc = 2 * k + c
                source[kc, :depth, tile] = main[c]
                edge = jnp.where(is_high, over[c], under[c])
                source[kc, depth:, tile] = edge
                fields[0][kc, :depth, shifted] = main[2 + c]
                f_over, f_under = over[2 + c], under[2 + c]
                fields[0][kc, depth:, shifted] = jnp.where(is_high, f_over, f_under)
                fifth_over = pltpu.roll(f_over, HALO - 1, 0) - pltpu.roll(f_under, HALO - 1, 0)
                fifth_under = pltpu.roll(f_under, 1, 0) - pltpu.roll(f_over, 1, 0)
                fix = jnp.where(edge_rows == half - 1, fifth_over, 0.0) + jnp.where(
                    edge_rows == half, fifth_under, 0.0
                )
                source_edge[kc, :, tile] = edge + fix

    def near(before, v, after):
        along_x = pltpu.roll(v + jnp.where(upper_half, before, after), GY, 1)
        left = jnp.where(not_first, pltpu.roll(v, 1, 1), 0.0)
        right = jnp.where(not_last, pltpu.roll(v, LANES - 1, 1), 0.0)
        along_z = pltpu.roll(v, 1, 0) + pltpu.roll(v, tall - 1, 0)
        return along_x + left + right + along_z

    kept = 1.0 - relaxation

    def sweep(number, start, tiles):
        old = (number - 1) % 2
        final = number == SWEEPS - 1
        rows = depth if final else tall
        s_re = [scale_re[:rows, tile_of(start + j)] for j in range(tiles)]
        s_im = [scale_im[:rows, tile_of(start + j)] for j in range(tiles)]

        def pulled(kc):
            v = [fields[old][kc, :, tile_of(start + j)] for j in range(tiles + 2)]
            gives = []
            for j in range(tiles):
                tile = tile_of(start + j)
                if number == 1:
                    added = jnp.concatenate([source[kc, :depth, tile], source_edge[kc, :, tile]], 0)
                else:
                    added = source[kc, :rows, tile]
                n = near(v[j], v[j + 1], v[j + 2])
                gives.append((kept * v[j + 1][:rows], n[:rows] + added))
            return gives

        for k in range(owned):
            real = pulled(2 * k)
            imag = pulled(2 * k + 1)
            new = []
            for j in range(tiles):
                (v_re, n_re), (v_im, n_im) = real[j], imag[j]
                new.append(
                    (
                        v_re + (s_re[j] * n_re - s_im[j] * n_im),
                        v_im + (s_re[j] * n_im + s_im[j] * n_re),
                    )
                )
            for j in range(tiles):
                for c in range(2):
                    if final:
                        out[c, k, :, tile_of(start + j)] = new[j][c]
                    else:
                        fields[1 - old][2 * k + c, :, tile_of(start + j + 1)] = new[j][c]

    def run_sweep(low, high, number):
        groups = (high - low) // GROUP

        def many(g, carry):
            sweep(number, low + g * GROUP, GROUP)
            return carry

        if groups:
            lax.fori_loop(0, groups, many, 0)
        rest = (high - low) % GROUP
        if rest:
            sweep(number, high - rest, rest)

    def run(low, high, work, size):
        def many(g, carry):
            for j in range(size):
                work(low + g * size + j)
            return carry

        lax.fori_loop(0, (high - low) // size, many, 0)

    def compute(turn):
        def wait_edge(mine, theirs, up):
            theirs.wait_recv()

        each(lambda up: edge_copy(up, turn), wait_edge)
        run(turn * per_part, (turn + 1) * per_part, functools.partial(begin, turn), 2)
        for number in range(1, SWEEPS):
            low = 0 if turn == 0 else max(turn * per_part - number, 0)
            high = cells // LANES if turn == rounds - 1 else max((turn + 1) * per_part - number, 0)
            if high > low:
                run_sweep(low, high, number)

    for turn in range(rounds):
        for mask in order:
            second_copy(turn, mask).wait_recv()
        run(turn * per_part, (turn + 1) * per_part, functools.partial(pack, turn), 4)

        def start_edge(mine, theirs, up):
            mine.start()

        each(lambda up: edge_copy(up, turn), start_edge)
        if turn > 0:
            compute(turn - 1)
    compute(rounds - 1)

    for turn in range(rounds):
        for mask in order:
            first_copy(turn, mask).wait_send()
            second_copy(turn, mask).wait_send()

        def end_edge(mine, theirs, up):
            mine.wait_send()

        each(lambda up: edge_copy(up, turn), end_edge)


def local(n, slabs, green_fields, pair_list, pair_values, noise_map, wave_square, station_cell):
    _, owned, depth, cells = green_fields.shape
    count = owned * n
    rounds = min(ROUNDS, cells // (n * LANES))
    width = cells // (n * rounds)
    tall = depth + HALO
    size = 2 * count * depth
    vmem = pl.BlockSpec(memory_space=pltpu.VMEM)
    hbm = pl.BlockSpec(memory_space=pltpu.HBM)
    dma = pltpu.SemaphoreType.DMA
    return pl.pallas_call(
        functools.partial(kernel, n, slabs, rounds),
        out_shape=jax.ShapeDtypeStruct((2, owned, depth, cells), f32),
        in_specs=[hbm] * 6,
        out_specs=vmem,
        scratch_shapes=[
            pltpu.VMEM(pair_list.shape[::-1], jnp.int32),
            pltpu.VMEM(pair_values.shape, f32),
            pltpu.VMEM((1, owned), jnp.int32),
            pltpu.VMEM((depth, cells), f32),
            pltpu.VMEM((depth, cells), f32),
            pltpu.VMEM((rounds, 2, count, depth, width), bf16),
            pltpu.VMEM((rounds, 2, count, depth, width), bf16),
            pltpu.VMEM((rounds, n, 2, owned, depth, width), bf16),
            pltpu.VMEM((size, size), bf16),
            pltpu.VMEM((2, owned, 2 * HALO, cells), bf16),
            pltpu.VMEM((2, owned, 2 * HALO, cells), bf16),
            pltpu.VMEM((2, 2, HALO, cells), f32),
            pltpu.VMEM((2 * owned, tall, cells), f32),
            pltpu.VMEM((2 * owned, HALO, cells), f32),
            pltpu.VMEM((tall, cells), f32),
            pltpu.VMEM((tall, cells), f32),
            pltpu.VMEM((2, 2, HALO, cells), f32),
            pltpu.VMEM((2 * owned, tall, cells + 2 * LANES), f32),
            pltpu.VMEM((2 * owned, tall, cells + 2 * LANES), f32),
            dma((rounds, n)),
            dma((rounds, n)),
            dma((rounds, n)),
            dma((rounds, n)),
            dma((2, rounds)),
            dma((2, rounds)),
            dma((2, 2)),
            dma((2, 2)),
            dma((rounds,)),
            dma((5,)),
        ],
        compiler_params=pltpu.CompilerParams(
            collective_id=0, has_side_effects=True, vmem_limit_bytes=62 * 1024 * 1024
        ),
    )(green_fields, pair_list.T, pair_values, noise_map, wave_square, station_cell[None, :])


def solution(mesh):
    placed = (P(None, "sta", "slab", None), P(), P(), P("slab", None), P("slab", None), P("sta"))
    return jax.shard_map(
        functools.partial(local, mesh.shape["sta"], mesh.shape["slab"]),
        mesh=mesh,
        in_specs=placed,
        out_specs=P(None, "sta", "slab", None),
        check_vma=False,
    )
```
